32 devices in a mesh: tm: 16 (over z, y, core), mp: 2 (over x).
Axes of the slice: x: 2, y: 2, z: 4, core: 2. Of those that a mesh axis runs over, the one named last changes fastest.
Arguments:
- latent_picture_tokens: bfloat16 [32, 384, 768], P(('tm', 'mp')), may hold values from -6 to 6
- mixing_rescale_factor: float32 [2, 768], replicated, may hold values from 0.1 to 1.9
- joint_lookup_matrix: bfloat16 [2, 768, 1280], P(None, None, 'mp')
- score_scaling: float32 [2, 6], replicated, may hold values from 1 to 24
- mixing_return_matrix: bfloat16 [2, 768, 768], P(None, 'mp'), may hold values from -0.21875 to 0.21875
- perceptron_rescale_factor: float32 [2, 768], replicated, may hold values from 0.1 to 1.9
- widening_matrix: bfloat16 [2, 768, 1536], P(None, None, 'mp'), may hold values from -0.21875 to 0.21875
- narrowing_matrix: bfloat16 [2, 1536, 768], P(None, 'mp'), may hold values from -0.15625 to 0.15625
Outputs:
- result: bfloat16 [32, 384, 768], P(('tm', 'mp'))
The draws below stay inside these ranges and needn't reach their ends.
All inputs are finite; a program needn't handle non-finite values.
Results may differ from the reference program's by a relative error of at most 0.033.
Values may be sent and summed in bfloat16 or wider, within the bound.
A program may use at most 128 MiB of HBM per device.

```python
import math
import jax
import jax.numpy as jnp
from jax import lax

MODEL_WIDTH = 768
HQ = 6
SHARED_GROUPS = 2
HEAD_SIZE = 128
ASKERS_IN_GROUP = 3
QKV = 1280
FF = 1536
S = 384
LAYER_COUNT = 2
FRAMES = 32


def draw_latent_picture_tokens(key, part):
    second = jax.random.fold_in(key, 1)
    own = jax.random.normal(second, (FRAMES, S, MODEL_WIDTH), jnp.float32)
    content_vectors = own
    return jnp.clip(content_vectors, -6.0, 6.0).astype(jnp.bfloat16)


def draw_joint_lookup_matrix(key, part):
    content_vectors = jax.random.truncated_normal(key, -4.0, 4.0, (LAYER_COUNT, MODEL_WIDTH, QKV), jnp.float32) / math.sqrt(MODEL_WIDTH)
    return content_vectors.astype(jnp.bfloat16)


def draw_score_scaling(key, part):
    spread = jax.random.uniform(key, (LAYER_COUNT, HQ), jnp.float32)
    content_vectors = jnp.exp(spread * math.log(4.0))
    return content_vectors.astype(jnp.float32)


def shard_levels(rng, shape, pieces, smallest, high):
    loudness, own = 1.0, jax.random.fold_in(rng, 6)
    for position, parts in pieces:
        heights = jnp.exp(jax.random.uniform(jax.random.fold_in(own, position), (parts,), jnp.float32, smallest / len(pieces), high / len(pieces)))
        loudness = loudness * jnp.repeat(heights, shape[position] // parts).reshape([-1 if axis == position else 1 for axis in range(len(shape))])
    return loudness


def centred(key, extent, deviation, bound, pieces=(), kind=jnp.bfloat16):
    drawn = deviation * jax.random.normal(key, extent, jnp.float32)
    if pieces:
        drawn = drawn * shard_levels(key, extent, pieces, -0.22, 0.18)
    return jnp.clip(drawn, -bound, bound).astype(kind)


def setup_inputs(seed: int = 0) -> dict:
    arg_keys = jax.random.split(jax.random.key(seed), 9)
    return {
        "latent_picture_tokens": draw_latent_picture_tokens(jax.random.fold_in(arg_keys[8], 71), 0),
        "mixing_rescale_factor": jnp.clip(1.0 + 0.18 * jax.random.normal(arg_keys[1], (LAYER_COUNT, MODEL_WIDTH), jnp.float32), 0.1, 1.9),
        "joint_lookup_matrix": draw_joint_lookup_matrix(jax.random.fold_in(arg_keys[8], 71), 0),
        "score_scaling": draw_score_scaling(jax.random.fold_in(arg_keys[8], 71), 0),
        "mixing_return_matrix": centred(arg_keys[4], (LAYER_COUNT, HQ * HEAD_SIZE, MODEL_WIDTH), (HQ * HEAD_SIZE) ** -0.5, 0.21875, ((1, 2),)),
        "perceptron_rescale_factor": jnp.clip(1.0 + 0.18 * jax.random.normal(arg_keys[5], (LAYER_COUNT, MODEL_WIDTH), jnp.float32), 0.1, 1.9),
        "widening_matrix": centred(arg_keys[6], (LAYER_COUNT, MODEL_WIDTH, FF), MODEL_WIDTH ** -0.5, 0.21875, ((2, 2),)),
        "narrowing_matrix": centred(arg_keys[7], (LAYER_COUNT, FF, MODEL_WIDTH), FF ** -0.5, 0.15625, ((1, 2),)),
    }


def rms_rows(x, gain):
    content_vectors = x.astype(jnp.float32)
    scale = lax.rsqrt(lax.optimization_barrier(jnp.mean(content_vectors * content_vectors, axis=-1, keepdims=True)) + 1e-06)
    return content_vectors * scale * gain.astype(jnp.float32)

def head_norm(t):
    return t * lax.rsqrt(lax.optimization_barrier(jnp.mean(t * t, axis=-1, keepdims=True)) + 1e-06)

def separate_subspaces(flat_vectors, groups, temps):
    count = flat_vectors.shape[0]
    reshaped_rows = flat_vectors.reshape(count, S, groups, ASKERS_IN_GROUP + 2, HEAD_SIZE)
    asker_vectors = head_norm(reshaped_rows[:, :, :, :ASKERS_IN_GROUP, :]) * temps[None, None, :, :, None] / math.sqrt(HEAD_SIZE)
    matcher_vectors = head_norm(reshaped_rows[:, :, :, ASKERS_IN_GROUP, :])
    content_vectors = reshaped_rows[:, :, :, ASKERS_IN_GROUP + 1, :]
    return (asker_vectors.astype(jnp.bfloat16), matcher_vectors.astype(jnp.bfloat16), content_vectors.astype(jnp.bfloat16))

def attend(asker_vectors, matcher_vectors, content_vectors, prior_k, prior_v, anchor_k, anchor_v, frame_ids):
    qf = asker_vectors.astype(jnp.float32)
    own = jnp.einsum('fsgrd,ftgd->fgrst', qf, matcher_vectors.astype(jnp.float32))
    prior = jnp.einsum('fsgrd,ftgd->fgrst', qf, prior_k.astype(jnp.float32))
    anchor = jnp.einsum('fsgrd,tgd->fgrst', qf, anchor_k.astype(jnp.float32))
    lowest = jnp.float32(-1e+30)
    prior = jnp.where((frame_ids >= 1)[:, None, None, None, None], prior, lowest)
    anchor = jnp.where((frame_ids >= 2)[:, None, None, None, None], anchor, lowest)
    top = jnp.maximum(jnp.maximum(lax.optimization_barrier(jnp.max(own, axis=-1, keepdims=True)), lax.optimization_barrier(jnp.max(prior, axis=-1, keepdims=True))), lax.optimization_barrier(jnp.max(anchor, axis=-1, keepdims=True)))
    e_own = jnp.exp(own - top)
    e_prior = jnp.exp(prior - top)
    e_anchor = jnp.exp(anchor - top)
    total = lax.optimization_barrier(jnp.sum(e_own, axis=-1, keepdims=True)) + lax.optimization_barrier(jnp.sum(e_prior, axis=-1, keepdims=True)) + lax.optimization_barrier(jnp.sum(e_anchor, axis=-1, keepdims=True))
    p_own = (e_own / total).astype(jnp.bfloat16).astype(jnp.float32)
    p_prior = (e_prior / total).astype(jnp.bfloat16).astype(jnp.float32)
    p_anchor = (e_anchor / total).astype(jnp.bfloat16).astype(jnp.float32)
    mixed = jnp.einsum('fgrst,ftgd->fsgrd', p_own, content_vectors.astype(jnp.float32))
    mixed = mixed + jnp.einsum('fgrst,ftgd->fsgrd', p_prior, prior_v.astype(jnp.float32))
    mixed = mixed + jnp.einsum('fgrst,tgd->fsgrd', p_anchor, anchor_v.astype(jnp.float32))
    count = asker_vectors.shape[0]
    return mixed.astype(jnp.bfloat16).reshape(count, S, -1)

def reference(latent_picture_tokens, mixing_rescale_factor, joint_lookup_matrix, score_scaling, mixing_return_matrix, perceptron_rescale_factor, widening_matrix, narrowing_matrix):
    state = latent_picture_tokens
    for depth_position in range(LAYER_COUNT):
        normed = rms_rows(state, mixing_rescale_factor[depth_position]).astype(jnp.bfloat16)
        flat_vectors = jnp.einsum('fsd,dc->fsc', normed.astype(jnp.float32), joint_lookup_matrix[depth_position].astype(jnp.float32))
        asker_vectors, matcher_vectors, content_vectors = separate_subspaces(flat_vectors, SHARED_GROUPS, score_scaling[depth_position].reshape(SHARED_GROUPS, ASKERS_IN_GROUP))

        def one_frame(index):
            before = jnp.maximum(index - 1, 0)
            result_frame = attend(asker_vectors[index][None], matcher_vectors[index][None], content_vectors[index][None], matcher_vectors[before][None], content_vectors[before][None], matcher_vectors[0], content_vectors[0], index[None])
            return result_frame[0]
        heads_out = lax.map(one_frame, jnp.arange(FRAMES, dtype=jnp.int32))
        mixed = jnp.einsum('fsc,cd->fsd', heads_out.astype(jnp.float32), mixing_return_matrix[depth_position].astype(jnp.float32))
        state = (state.astype(jnp.float32) + mixed).astype(jnp.bfloat16)
        normed2 = rms_rows(state, perceptron_rescale_factor[depth_position]).astype(jnp.bfloat16)
        hidden = jnp.einsum('fsd,dc->fsc', normed2.astype(jnp.float32), widening_matrix[depth_position].astype(jnp.float32))
        active = jax.nn.gelu(hidden, approximate=True).astype(jnp.bfloat16)
        update = jnp.einsum('fsc,cd->fsd', active.astype(jnp.float32), narrowing_matrix[depth_position].astype(jnp.float32))
        state = (state.astype(jnp.float32) + update).astype(jnp.bfloat16)
    return state
```

```python
import math

import jax
import jax.numpy as jnp
from jax import lax
from jax.experimental import pallas as pl
from jax.experimental.pallas import tpu as pltpu
from jax.sharding import PartitionSpec as P

D = 128
R = 3
S = 384
XCH = 4
MESH = pl.DeviceIdType.MESH
F32, BF16 = jnp.float32, jnp.bfloat16


def norm_rows(x, gain):
    x = x.astype(F32)
    scale = lax.rsqrt(jnp.mean(x * x, axis=-1, keepdims=True) + 1e-06)
    return (x * scale * gain).astype(BF16)


def head_norm(t):
    return t * lax.rsqrt(jnp.mean(t * t, axis=-1, keepdims=True) + 1e-06)


def dot(a, b):
    return jnp.dot(a, b, preferred_element_type=F32)


def kernel(
    T,
    x_ref, ga_ref, qkv_ref, temp_ref, out_ref, gf_ref, up_ref, down_ref,
    y_ref,
    wq, wo, wu, wd, x0, st, h, q, kc, vc, o, act,
    ws, wr, xsend, xrecv, ksend, krecv,
):
    tm, mp = lax.axis_index("tm"), lax.axis_index("mp")
    c, yb, zb = lax.rem(tm, 2), lax.rem(tm // 2, 2), lax.rem(tm // 4, 2)
    frame = tm * 2 + mp
    xdev = (tm, 1 - mp)
    cdev = (tm + 1 - 2 * c, mp)
    ydev = (tm + 2 - 4 * yb, mp)
    zdev = (tm + 4 - 8 * zb, mp)
    has_next = frame < 2 * T - 1
    has_prev = frame > 0
    ndev = (jnp.minimum(tm + mp, T - 1), 1 - mp)
    chain = jnp.logical_and(lax.rem(tm, 4) == 0, mp == 0)
    chain_next = jnp.logical_and(chain, tm + 4 < T)
    znext = jnp.minimum(tm + 4, T - 4)

    barrier = pltpu.get_barrier_semaphore()
    for dev in (xdev, cdev, ydev, zdev):
        pl.semaphore_signal(barrier, inc=1, device_id=dev, device_id_type=MESH)
    diag_up = jnp.logical_and(mp == 1, tm < T - 1)
    diag_down = jnp.logical_and(mp == 0, tm > 0)
    z_up = jnp.logical_and(jnp.logical_and(chain, zb == 1), tm + 4 < T)
    z_down = jnp.logical_and(jnp.logical_and(chain, zb == 0), tm > 0)

    def greet(cond, dev):
        @pl.when(cond)
        def _():
            pl.semaphore_signal(barrier, inc=1, device_id=dev, device_id_type=MESH)

    greet(diag_up, (jnp.minimum(tm + 1, T - 1), 0))
    greet(diag_down, (jnp.maximum(tm - 1, 0), 1))
    greet(z_up, (znext, 0))
    greet(z_down, (jnp.maximum(tm - 4, 0), 0))
    peers = jnp.int32(4)
    for cond in (diag_up, diag_down, z_up, z_down):
        peers = peers + jnp.where(cond, 1, 0)
    pl.semaphore_wait(barrier, peers)

    mats = []
    for l in range(2):
        mats += [(qkv_ref, wq, l), (out_ref, wo, l), (up_ref, wu, l), (down_ref, wd, l)]

    def wcopy(m, stage):
        src, dst, l = mats[m]
        rows = dst.shape[1] // 8
        y_first = m % 2 == 0
        e = c * 4 + (zb * 2 + yb if y_first else yb * 2 + zb)
        if stage == 0:
            at = pl.ds(pl.multiple_of(e * rows, rows), rows)
            sref, dev = src.at[l, at], xdev
        else:
            n = (0, 1, 2, 4)[stage]
            lead = (e, e, c * 4 + (zb if y_first else yb) * 2, c * 4)[stage]
            at = pl.ds(pl.multiple_of(lead * rows, rows), n * rows)
            sref = dst.at[l, at]
            dev = (None, ydev if y_first else zdev, zdev if y_first else ydev, cdev)[stage]
        return pltpu.make_async_remote_copy(
            src_ref=sref, dst_ref=dst.at[l, at], send_sem=ws.at[m, stage],
            recv_sem=wr.at[m, stage], device_id=dev, device_id_type=MESH,
        )

    def tick(t):
        if t + 2 < 8:
            wcopy(t + 2, 0).start()
        for stage in (1, 2, 3):
            m = t + 1 - stage
            if 0 <= m < 8:
                wcopy(m, stage - 1).wait_recv()
                wcopy(m, stage).start()

    def arrived(m):
        wcopy(m, 3).wait_recv()

    step = S // XCH
    children = (
        (chain_next, (znext, 0)),
        (chain, (tm + 2 - 4 * yb, 0)),
        (jnp.logical_and(c == 0, mp == 0), (tm, 1)),
        (c == 0, cdev),
    )

    def xcopy(k, child, src):
        at = pl.ds(k * step, step)
        return pltpu.make_async_remote_copy(
            src_ref=src.at[at], dst_ref=x0.at[at], send_sem=xsend.at[k, child],
            recv_sem=xrecv.at[k], device_id=children[child][1], device_id_type=MESH,
        )

    def each_child(k, what):
        for i, (cond, _) in enumerate(children):
            @pl.when(cond)
            def _(i=i):
                what(xcopy(k, i, x0))

    def xpump(k):
        @pl.when(frame > 0)
        def _():
            xcopy(k, 3, x0).wait_recv()
        each_child(k, lambda d: d.start())

    def kcopy(l, slot, i):
        buf = (kc, vc)[i]
        return pltpu.make_async_remote_copy(
            src_ref=buf.at[l, slot, pl.ds(0, S)], dst_ref=buf.at[l, 1 - slot, pl.ds(2 * S, S)],
            send_sem=ksend.at[l, slot, i], recv_sem=krecv.at[l, 1 - slot, i],
            device_id=ndev, device_id_type=MESH,
        )

    def ksend_slot(l, slot):
        @pl.when(has_next)
        def _():
            kcopy(l, slot, 0).start()
            kcopy(l, slot, 1).start()

        @pl.when(jnp.logical_not(has_prev))
        def _():
            kc[l, slot, 2 * S :, :] = kc[l, slot, :S, :]
            vc[l, slot, 2 * S :, :] = vc[l, slot, :S, :]

    def kwait(l):
        @pl.when(has_prev)
        def _():
            for slot in range(2):
                for i in range(2):
                    kcopy(l, slot, i).wait_recv()

    def project(l, slot, f, only_kv=False):
        w = (qkv_ref, wq)[slot]
        group = mp if slot == 0 else 1 - mp
        a = h[f * S : (f + 1) * S, :]
        lo = R * D if only_kv else 0
        flat = dot(a, w[l, :, lo:])
        if not only_kv:
            for r in range(R):
                t = temp_ref[l, group * R + r] * (1.0 / math.sqrt(D))
                q[f * 6 + slot * R + r] = (head_norm(flat[:, r * D : (r + 1) * D]) * t).astype(BF16)
        kc[l, slot, f * S : (f + 1) * S, :] = head_norm(flat[:, R * D - lo : (R + 1) * D - lo]).astype(BF16)
        vc[l, slot, f * S : (f + 1) * S, :] = flat[:, (R + 1) * D - lo :].astype(BF16)

    col = lax.broadcasted_iota(jnp.int32, (1, 3 * S), 1)
    keep = (col < S) | ((col < 2 * S) & (frame >= 2)) | ((col >= 2 * S) & (frame >= 1))
    bias = jnp.where(keep, 0.0, -1e30).astype(F32)

    def attend(l, f):
        def group(slot, carry):
            for r in range(R):
                qq = q[f * 6 + slot * R + r]
                kk, vv = (kc[l, slot], vc[l, slot]) if f == 0 else (kc[l, slot, S : 2 * S, :], vc[l, slot, S : 2 * S, :])
                s = lax.dot_general(qq, kk, (((1,), (1,)), ((), ())), preferred_element_type=F32)
                if f == 0:
                    s = s + bias
                e = jnp.exp(s - jnp.max(s, axis=-1, keepdims=True))
                total = jnp.sum(e, axis=-1, keepdims=True)
                res = dot(e.astype(BF16), vv) / total
                at = pl.ds(pl.multiple_of((slot * R + r) * D, D), D)
                o[f * S : (f + 1) * S, at] = res.astype(BF16)
            return carry
        lax.fori_loop(0, 2, group, 0)

    half = R * D
    width = up_ref.shape[2]

    def mix(l, f, state):
        rows = slice(f * S, (f + 1) * S)
        upd = dot(o[rows, :half], out_ref[l]) + dot(o[rows, half:], wo[l])
        new = (state.astype(F32) + upd).astype(BF16)
        st[rows, :] = new
        h[rows, :] = norm_rows(new, gf_ref[l : l + 1, :])

    def widen(l, n, slot):
        w = (up_ref, wu)[slot]
        for f in range(n):
            rows = slice(f * S, (f + 1) * S)
            hid = dot(h[rows, :], w[l])
            act[rows, slot * width : (slot + 1) * width] = jax.nn.gelu(hid, approximate=True).astype(BF16)

    def narrow(l, f):
        rows = slice(f * S, (f + 1) * S)
        upd = dot(act[rows, :width], down_ref[l]) + dot(act[rows, width:], wd[l])
        return (st[rows, :].astype(F32) + upd).astype(BF16)

    @pl.when(frame == 0)
    def _():
        x0[...] = x_ref[...]
        for k in range(XCH):
            xpump(k)

    early = jnp.logical_and(chain, frame > 0)
    wcopy(0, 0).start()
    wcopy(1, 0).start()
    h[:S, :] = norm_rows(x_ref[...], ga_ref[0:1, :])
    project(0, 0, 0)
    ksend_slot(0, 0)
    for t in range(3):
        @pl.when(early)
        def _(t=t):
            xpump(t)
        tick(t)

    @pl.when(early)
    def _():
        xpump(3)
    arrived(0)
    project(0, 1, 0)
    ksend_slot(0, 1)
    tick(3)

    @pl.when(jnp.logical_not(chain))
    def _():
        for k in range(XCH):
            xpump(k)
    h[S:, :] = norm_rows(x0[...], ga_ref[0:1, :])
    project(0, 0, 1)
    project(0, 1, 1)
    tick(4)
    attend(0, 1)
    tick(5)
    kwait(0)
    attend(0, 0)
    arrived(1)
    mix(0, 1, x0[...])
    mix(0, 0, x_ref[...])
    tick(6)
    arrived(2)
    widen(0, 2, 0)
    widen(0, 2, 1)
    tick(7)
    arrived(3)
    for f in range(2):
        new = narrow(0, f)
        st[f * S : (f + 1) * S, :] = new
        h[f * S : (f + 1) * S, :] = norm_rows(new, ga_ref[1:2, :])

    arrived(4)
    project(1, 0, 0)
    ksend_slot(1, 0)
    project(1, 1, 0)
    ksend_slot(1, 1)
    tick(8)
    project(1, 0, 1, only_kv=True)
    project(1, 1, 1, only_kv=True)
    tick(9)
    kwait(1)
    attend(1, 0)
    arrived(5)
    mix(1, 0, st[:S, :])
    arrived(6)
    widen(1, 1, 0)
    widen(1, 1, 1)
    arrived(7)
    y_ref[...] = narrow(1, 0)

    for m in range(8):
        for stage in range(4):
            wcopy(m, stage).wait_send()
    for k in range(XCH):
        each_child(k, lambda d: d.wait_send())

    @pl.when(has_next)
    def _():
        for l in range(2):
            for slot in range(2):
                for i in range(2):
                    kcopy(l, slot, i).wait_send()


def solution(mesh):
    T = mesh.shape["tm"]

    def shards(x, ga, qkv, temps, out, gf, up, down):
        width = x.shape[2]
        vmem = pl.BlockSpec(memory_space=pltpu.VMEM)
        smem = pl.BlockSpec(memory_space=pltpu.SMEM)

        def body(*refs):
            kernel(T, *refs)

        y = pl.pallas_call(
            body,
            out_shape=jax.ShapeDtypeStruct((S, width), BF16),
            in_specs=[vmem, vmem, vmem, smem, vmem, vmem, vmem, vmem],
            out_specs=vmem,
            scratch_shapes=[
                pltpu.VMEM(qkv.shape, BF16),
                pltpu.VMEM(out.shape, BF16),
                pltpu.VMEM(up.shape, BF16),
                pltpu.VMEM(down.shape, BF16),
                pltpu.VMEM((S, width), BF16),
                pltpu.VMEM((2 * S, width), BF16),
                pltpu.VMEM((2 * S, width), BF16),
                pltpu.VMEM((12, S, D), BF16),
                pltpu.VMEM((2, 2, 3 * S, D), BF16),
                pltpu.VMEM((2, 2, 3 * S, D), BF16),
                pltpu.VMEM((2 * S, 2 * R * D), BF16),
                pltpu.VMEM((2 * S, 2 * up.shape[2]), BF16),
                pltpu.SemaphoreType.DMA((8, 4)),
                pltpu.SemaphoreType.DMA((8, 4)),
                pltpu.SemaphoreType.DMA((XCH, 4)),
                pltpu.SemaphoreType.DMA((XCH,)),
                pltpu.SemaphoreType.DMA((2, 2, 2)),
                pltpu.SemaphoreType.DMA((2, 2, 2)),
            ],
            compiler_params=pltpu.CompilerParams(
                collective_id=0, has_side_effects=True, vmem_limit_bytes=56 * 1024 * 1024
            ),
        )(x.reshape(S, width), ga, qkv, temps, out, gf, up, down)
        return y.reshape(x.shape)

    in_specs = (
        P(("tm", "mp"), None, None),
        P(),
        P(None, None, "mp"),
        P(),
        P(None, "mp", None),
        P(),
        P(None, None, "mp"),
        P(None, "mp", None),
    )
    return jax.shard_map(
        shards, mesh=mesh, in_specs=in_specs, out_specs=P(("tm", "mp"), None, None), check_vma=False
    )
```

```python
import math

import jax
import jax.numpy as jnp
from jax import lax
from jax.experimental import pallas as pl
from jax.experimental.pallas import tpu as pltpu
from jax.sharding import PartitionSpec as P

D = 128
R = 3
S = 384
XCH = 4
MESH = pl.DeviceIdType.MESH
F32, BF16 = jnp.float32, jnp.bfloat16


def norm_rows(x, gain):
    x = x.astype(F32)
    scale = lax.rsqrt(jnp.mean(x * x, axis=-1, keepdims=True) + 1e-06)
    return (x * scale * gain).astype(BF16)


def head_norm(t):
    return t * lax.rsqrt(jnp.mean(t * t, axis=-1, keepdims=True) + 1e-06)


def dot(a, b):
    return jnp.dot(a, b, preferred_element_type=F32)


def kernel(
    T,
    x_ref, ga_ref, qkv_hbm, temp_ref, out_hbm, gf_ref, up_hbm, down_hbm,
    y_ref,
    qkv_ref, out_ref, up_ref, down_ref, wq, wo, wu, wd,
    x0, st, h, q, kc, vc, o, act, top, total, acc,
    loaded, ws, wr, xsend, xrecv, ksend, krecv, asend, arecv,
):
    tm, mp = lax.axis_index("tm"), lax.axis_index("mp")
    c, yb, zb = lax.rem(tm, 2), lax.rem(tm // 2, 2), lax.rem(tm // 4, 2)
    frame = tm * 2 + mp
    xdev = (tm, 1 - mp)
    cdev = (tm + 1 - 2 * c, mp)
    ydev = (tm + 2 - 4 * yb, mp)
    zdev = (tm + 4 - 8 * zb, mp)
    has_next = frame < 2 * T - 1
    has_prev = frame > 0
    ndev = (jnp.minimum(tm + mp, T - 1), 1 - mp)
    chain = jnp.logical_and(lax.rem(tm, 4) == 0, mp == 0)
    chain_next = jnp.logical_and(chain, tm + 4 < T)
    znext = jnp.minimum(tm + 4, T - 4)

    for m in range(8):
        src, dst, l = ((qkv_hbm, qkv_ref), (out_hbm, out_ref), (up_hbm, up_ref), (down_hbm, down_ref))[m % 4] + (m // 4,)
        pltpu.make_async_copy(src.at[l], dst.at[l], loaded.at[m]).start()

    barrier = pltpu.get_barrier_semaphore()
    for dev in (xdev, cdev, ydev, zdev):
        pl.semaphore_signal(barrier, inc=1, device_id=dev, device_id_type=MESH)
    diag_up = jnp.logical_and(mp == 1, tm < T - 1)
    diag_down = jnp.logical_and(mp == 0, tm > 0)
    z_up = jnp.logical_and(jnp.logical_and(chain, zb == 1), tm + 4 < T)
    z_down = jnp.logical_and(jnp.logical_and(chain, zb == 0), tm > 0)

    def greet(cond, dev):
        @pl.when(cond)
        def _():
            pl.semaphore_signal(barrier, inc=1, device_id=dev, device_id_type=MESH)

    greet(diag_up, (jnp.minimum(tm + 1, T - 1), 0))
    greet(diag_down, (jnp.maximum(tm - 1, 0), 1))
    greet(z_up, (znext, 0))
    greet(z_down, (jnp.maximum(tm - 4, 0), 0))
    peers = jnp.int32(4)
    for cond in (diag_up, diag_down, z_up, z_down):
        peers = peers + jnp.where(cond, 1, 0)
    pl.semaphore_wait(barrier, peers)

    mats = []
    for l in range(2):
        mats += [(qkv_hbm, wq, l), (out_hbm, wo, l), (up_hbm, wu, l), (down_hbm, wd, l)]
    held = (qkv_ref, out_ref, up_ref, down_ref)

    def load(m):
        src, _, l = mats[m]
        return pltpu.make_async_copy(src.at[l], held[m % 4].at[l], loaded.at[m])

    def wcopy(m, stage):
        src, dst, l = mats[m]
        rows = dst.shape[1] // 8
        y_first = m % 2 == 0
        e = c * 4 + (zb * 2 + yb if y_first else yb * 2 + zb)
        if stage == 0:
            at = pl.ds(pl.multiple_of(e * rows, rows), rows)
            sref, dev = src.at[l, at], xdev
        else:
            n = (0, 1, 2, 4)[stage]
            lead = (e, e, c * 4 + (zb if y_first else yb) * 2, c * 4)[stage]
            at = pl.ds(pl.multiple_of(lead * rows, rows), n * rows)
            sref = dst.at[l, at]
            dev = (None, ydev if y_first else zdev, zdev if y_first else ydev, cdev)[stage]
        return pltpu.make_async_remote_copy(
            src_ref=sref, dst_ref=dst.at[l, at], send_sem=ws.at[m, stage],
            recv_sem=wr.at[m, stage], device_id=dev, device_id_type=MESH,
        )

    def tick(t):
        if t + 2 < 8:
            wcopy(t + 2, 0).start()
        for stage in (1, 2, 3):
            m = t + 1 - stage
            if 0 <= m < 8:
                wcopy(m, stage - 1).wait_recv()
                wcopy(m, stage).start()

    def arrived(m):
        wcopy(m, 3).wait_recv()

    step = S // XCH
    children = (
        (chain_next, (znext, 0)),
        (chain, (tm + 2 - 4 * yb, 0)),
        (jnp.logical_and(c == 0, mp == 0), (tm, 1)),
        (c == 0, cdev),
    )

    def xcopy(k, child, src):
        at = pl.ds(k * step, step)
        return pltpu.make_async_remote_copy(
            src_ref=src.at[at], dst_ref=x0.at[at], send_sem=xsend.at[k, child],
            recv_sem=xrecv.at[k], device_id=children[child][1], device_id_type=MESH,
        )

    def each_child(make, what):
        for i, (cond, _) in enumerate(children):
            @pl.when(cond)
            def _(i=i):
                what(make(i))

    def xpump(k):
        @pl.when(frame > 0)
        def _():
            xcopy(k, 3, x0).wait_recv()
        each_child(lambda i: xcopy(k, i, x0), lambda d: d.start())

    def acopy(piece, child):
        g, buf = piece // 2, (kc, vc)[piece % 2]
        here = g + mp - 2 * g * mp
        there = 1 - here if child == 2 else here
        at = pl.ds(S, S)
        return pltpu.make_async_remote_copy(
            src_ref=buf.at[1, here, at], dst_ref=buf.at[1, there, at], send_sem=asend.at[piece, child],
            recv_sem=arecv.at[piece], device_id=children[child][1], device_id_type=MESH,
        )

    def apump(piece):
        @pl.when(frame > 0)
        def _():
            acopy(piece, 3).wait_recv()
        each_child(lambda i: acopy(piece, i), lambda d: d.start())

    def kcopy(l, slot, i):
        buf = (kc, vc)[i]
        return pltpu.make_async_remote_copy(
            src_ref=buf.at[l, slot, pl.ds(0, S)], dst_ref=buf.at[l, 1 - slot, pl.ds(2 * S, S)],
            send_sem=ksend.at[l, slot, i], recv_sem=krecv.at[l, 1 - slot, i],
            device_id=ndev, device_id_type=MESH,
        )

    def ksend_slot(l, slot):
        @pl.when(has_next)
        def _():
            kcopy(l, slot, 0).start()
            kcopy(l, slot, 1).start()

    def kwait(l, slot):
        @pl.when(has_prev)
        def _():
            for i in range(2):
                kcopy(l, 1 - slot, i).wait_recv()

    def project(l, slot, f, only_kv=False, h0=None):
        w = (qkv_ref, wq)[slot]
        group = mp if slot == 0 else 1 - mp
        a = h[...] if f == 0 else h0
        lo = R * D if only_kv else 0
        flat = dot(a, w[l, :, lo:])
        if not only_kv:
            for r in range(R):
                t = temp_ref[l, group * R + r] * (1.0 / math.sqrt(D))
                q[slot * R + r] = (head_norm(flat[:, r * D : (r + 1) * D]) * t).astype(BF16)
        kc[l, slot, f * S : (f + 1) * S, :] = head_norm(flat[:, R * D - lo : (R + 1) * D - lo]).astype(BF16)
        vc[l, slot, f * S : (f + 1) * S, :] = flat[:, (R + 1) * D - lo :].astype(BF16)

    col = lax.broadcasted_iota(jnp.int32, (1, 2 * S), 1)
    bias = jnp.where((col >= S) | (frame >= 2), 0.0, -1e30).astype(F32)

    def scores(qq, kk):
        return lax.dot_general(qq, kk, (((1,), (1,)), ((), ())), preferred_element_type=F32)

    def own_part(l, slot):
        kk, vv = kc[l, slot, :S, :], vc[l, slot, :S, :]
        for r in range(R):
            i = slot * R + r
            s = scores(q[i], kk)
            m = jnp.max(s, axis=-1, keepdims=True)
            e = jnp.exp(s - m)
            top[i] = m
            total[i] = jnp.sum(e, axis=-1, keepdims=True)
            acc[i] = dot(e.astype(BF16), vv)

    def other_part(l, slot):
        @pl.when(has_prev)
        def _():
            kk, vv = kc[l, slot, S:, :], vc[l, slot, S:, :]
            for r in range(R):
                i = slot * R + r
                s = scores(q[i], kk) + bias
                m = jnp.maximum(top[i], jnp.max(s, axis=-1, keepdims=True))
                e = jnp.exp(s - m)
                keep = jnp.exp(top[i] - m)
                sums = total[i] * keep + jnp.sum(e, axis=-1, keepdims=True)
                res = (acc[i] * keep + dot(e.astype(BF16), vv)) / sums
                o[:, i * D : (i + 1) * D] = res.astype(BF16)

        @pl.when(jnp.logical_not(has_prev))
        def _():
            for r in range(R):
                i = slot * R + r
                o[:, i * D : (i + 1) * D] = (acc[i] / total[i]).astype(BF16)

    half = R * D
    width = up_ref.shape[2]

    def mix(l, state):
        upd = dot(o[:, :half], out_ref[l]) + dot(o[:, half:], wo[l])
        new = (state.astype(F32) + upd).astype(BF16)
        st[...] = new
        h[...] = norm_rows(new, gf_ref[l : l + 1, :])

    def widen(l, slot):
        w = (up_ref, wu)[slot]
        hid = dot(h[...], w[l])
        act[:, slot * width : (slot + 1) * width] = jax.nn.gelu(hid, approximate=True).astype(BF16)

    def narrow(l):
        upd = dot(act[:, :width], down_ref[l]) + dot(act[:, width:], wd[l])
        return (st[...].astype(F32) + upd).astype(BF16)

    @pl.when(frame == 0)
    def _():
        x0[...] = x_ref[...]
        for k in range(XCH):
            xpump(k)

    early = jnp.logical_and(chain, frame > 0)
    late = jnp.logical_not(chain)
    wcopy(0, 0).start()
    wcopy(1, 0).start()
    h[...] = norm_rows(x_ref[...], ga_ref[0:1, :])
    load(0).wait()
    project(0, 0, 0)
    ksend_slot(0, 0)
    for t in range(3):
        @pl.when(early)
        def _(t=t):
            xpump(t)
        tick(t)
        if t == 0:
            own_part(0, 0)

    @pl.when(early)
    def _():
        xpump(3)
    arrived(0)
    project(0, 1, 0)
    ksend_slot(0, 1)
    tick(3)

    @pl.when(late)
    def _():
        xpump(0)
        xpump(1)
    own_part(0, 1)

    @pl.when(late)
    def _():
        xpump(2)
        xpump(3)
    tick(4)

    @pl.when(has_prev)
    def _():
        h0 = norm_rows(x0[...], ga_ref[0:1, :])
        project(0, 0, 1, only_kv=True, h0=h0)
        project(0, 1, 1, only_kv=True, h0=h0)
    kwait(0, 0)
    kwait(0, 1)
    tick(5)
    other_part(0, 0)
    tick(6)
    other_part(0, 1)
    load(1).wait()
    arrived(1)
    mix(0, x_ref[...])
    load(2).wait()
    widen(0, 0)
    tick(7)
    arrived(2)
    widen(0, 1)
    load(3).wait()
    arrived(3)
    new = narrow(0)
    st[...] = new
    h[...] = norm_rows(new, ga_ref[1:2, :])

    load(4).wait()
    project(1, 0, 0)
    ksend_slot(1, 0)

    @pl.when(frame == 0)
    def _():
        kc[1, 0, S : 2 * S, :] = kc[1, 0, :S, :]
        vc[1, 0, S : 2 * S, :] = vc[1, 0, :S, :]
        apump(0)
        apump(1)
    arrived(4)
    project(1, 1, 0)
    ksend_slot(1, 1)

    @pl.when(frame == 0)
    def _():
        kc[1, 1, S : 2 * S, :] = kc[1, 1, :S, :]
        vc[1, 1, S : 2 * S, :] = vc[1, 1, :S, :]
        apump(2)
        apump(3)
    tick(8)

    @pl.when(early)
    def _():
        apump(0)
        apump(1)
    own_part(1, 0)

    @pl.when(early)
    def _():
        apump(2)
        apump(3)

    @pl.when(late)
    def _():
        apump(0)
        apump(1)
    tick(9)
    own_part(1, 1)

    @pl.when(late)
    def _():
        apump(2)
        apump(3)
    kwait(1, 0)
    other_part(1, 0)
    kwait(1, 1)
    other_part(1, 1)
    load(5).wait()
    arrived(5)
    mix(1, st[...])
    load(6).wait()
    widen(1, 0)
    arrived(6)
    widen(1, 1)
    load(7).wait()
    arrived(7)
    y_ref[...] = narrow(1)

    for m in range(8):
        for stage in range(4):
            wcopy(m, stage).wait_send()
    for k in range(XCH):
        each_child(lambda i, k=k: xcopy(k, i, x0), lambda d: d.wait_send())
    for piece in range(4):
        each_child(lambda i, piece=piece: acopy(piece, i), lambda d: d.wait_send())

    @pl.when(has_next)
    def _():
        for l in range(2):
            for slot in range(2):
                for i in range(2):
                    kcopy(l, slot, i).wait_send()


def solution(mesh):
    T = mesh.shape["tm"]

    def shards(x, ga, qkv, temps, out, gf, up, down):
        width = x.shape[2]
        vmem = pl.BlockSpec(memory_space=pltpu.VMEM)
        hbm = pl.BlockSpec(memory_space=pl.ANY)
        smem = pl.BlockSpec(memory_space=pltpu.SMEM)

        def body(*refs):
            kernel(T, *refs)

        y = pl.pallas_call(
            body,
            out_shape=jax.ShapeDtypeStruct((S, width), BF16),
            in_specs=[vmem, vmem, hbm, smem, hbm, vmem, hbm, hbm],
            out_specs=vmem,
            scratch_shapes=[
                *[pltpu.VMEM(w.shape, BF16) for w in (qkv, out, up, down)] * 2,
                pltpu.VMEM((S, width), BF16),
                pltpu.VMEM((S, width), BF16),
                pltpu.VMEM((S, width), BF16),
                pltpu.VMEM((2 * R, S, D), BF16),
                pltpu.VMEM((2, 2, 3 * S, D), BF16),
                pltpu.VMEM((2, 2, 3 * S, D), BF16),
                pltpu.VMEM((S, 2 * R * D), BF16),
                pltpu.VMEM((S, 2 * up.shape[2]), BF16),
                pltpu.VMEM((2 * R, S, 1), F32),
                pltpu.VMEM((2 * R, S, 1), F32),
                pltpu.VMEM((2 * R, S, D), F32),
                pltpu.SemaphoreType.DMA((8,)),
                pltpu.SemaphoreType.DMA((8, 4)),
                pltpu.SemaphoreType.DMA((8, 4)),
                pltpu.SemaphoreType.DMA((XCH, 4)),
                pltpu.SemaphoreType.DMA((XCH,)),
                pltpu.SemaphoreType.DMA((2, 2, 2)),
                pltpu.SemaphoreType.DMA((2, 2, 2)),
                pltpu.SemaphoreType.DMA((4, 4)),
                pltpu.SemaphoreType.DMA((4,)),
            ],
            compiler_params=pltpu.CompilerParams(
                collective_id=0, has_side_effects=True, vmem_limit_bytes=56 * 1024 * 1024
            ),
        )(x.reshape(S, width), ga, qkv, temps, out, gf, up, down)
        return y.reshape(x.shape)

    in_specs = (
        P(("tm", "mp"), None, None),
        P(),
        P(None, None, "mp"),
        P(),
        P(None, "mp", None),
        P(),
        P(None, None, "mp"),
        P(None, "mp", None),
    )
    return jax.shard_map(
        shards, mesh=mesh, in_specs=in_specs, out_specs=P(("tm", "mp"), None, None), check_vma=False
    )
```
